32 devices in a mesh: grp: 2 (over y), row: 8 (over z, x), col: 2 (over core).
Axes of the slice: x: 2, y: 2, z: 4, core: 2. Of those that a mesh axis runs over, the one named last changes fastest.
Arguments:
- tokens: bfloat16 [128, 256, 180], P(('grp', 'row'), 'col'), parts along dimension 0, may hold values from -6 to 6
- grad_out: bfloat16 [128, 256, 180], P(('grp', 'row'), 'col'), parts along dimension 0, may hold values from -8 to 8
- regions: int32 [128, 256], P(('grp', 'row'), 'col'), parts along dimension 0, may hold values from 0 to 15, as said below
- ln_gain: float32 [180], replicated, may hold values from 0.1 to 1.9
- ln_offset: float32 [180], replicated, may hold values from -1.5 to 1.5
- qkv_weight: bfloat16 [180, 540], replicated, may hold values from -0.4375 to 0.4375
- qkv_bias: float32 [540], replicated, may hold values from -1.5 to 1.5
- proj_weight: bfloat16 [180, 180], replicated, may hold values from -0.4375 to 0.4375
- bias_table: float32 [225, 6], replicated, may hold values from -4 to 320
Outputs:
- d_tokens: bfloat16 [128, 256, 180], P(('grp', 'row'), 'col'), parts along dimension 0
- d_qkv_weight: float32 [360, 540], P('grp'), parts along dimension 0
- d_qkv_bias: float32 [1080], P('grp'), parts along dimension 0
- d_proj_weight: float32 [360, 180], P('grp'), parts along dimension 0
- d_bias_table: float32 [450, 6], P('grp'), parts along dimension 0
- d_ln_gain: float32 [360], P('grp'), parts along dimension 0
- d_ln_offset: float32 [360], P('grp'), parts along dimension 0
The draws below stay inside these ranges and needn't reach their ends.
There are 2 independent parts, one for each index of `grp`. The reference program is written for one: setup_inputs(seed, part) draws one part's arguments, and reference() takes and returns one part's arrays. A program takes and returns all parts, laid end to end along the dimension named above; an argument that names none is the same for every part. Nothing has to cross between parts.
Inputs may be any that keep to these rules, and one draw needn't show every extreme that they name: `regions`: A token attends only to tokens of its window with the same id. The map is a grid: the id is 4 a + b, where a, from 0 to 3, depends only on the token's row and b, from 0 to 3, only on its column.
All inputs are finite; a program needn't handle non-finite values.
Results may differ from the reference program's by a relative error of at most 0.0085.
Values may be sent and summed in bfloat16 or wider, within the bound.
A program may use at most 64 MiB of HBM per device.

```python
import jax
import jax.numpy as jnp
from jax import lax

C = 180
HEADS = 6
WIN = 8
SHIFT = 4
TABLE = 225
H = 64
W = 256


def draw_grad_out(key, part):
    key_one = jax.random.fold_in(key, 0)
    noise = jax.random.normal(key_one, (H, W, C), jnp.float32)
    values = noise
    return jnp.clip(values, -8.0, 8.0).astype(jnp.bfloat16)


def draw_regions(key, part):
    row_key, col_key = jax.random.split(key)
    row_flag = (jax.random.randint(row_key, (H,), 0, 16) == 0).astype(jnp.int32)
    row_flag = row_flag.at[0].set(0).at[1:4].set(1)
    col_flag = (jax.random.randint(col_key, (W,), 0, 16) == 0).astype(jnp.int32)
    col_flag = col_flag.at[0].set(0).at[1:4].set(1)
    row_band = jnp.cumsum(row_flag) % 4
    col_band = jnp.cumsum(col_flag) % 4
    return (row_band[:, None] * 4 + col_band[None, :]).astype(jnp.int32)


def draw_bias_table(key, part):
    values = jnp.clip(jax.random.normal(key, (TABLE, HEADS), jnp.float32), -4.0, 4.0)
    return values


def level_of(rng, dims, shards, smallest, top_value):
    def one(dim, shards_of):
        steps = jax.random.uniform(jax.random.fold_in(jax.random.fold_in(rng, 6), dim), (shards_of,), jnp.float32, smallest / len(shards), top_value / len(shards))
        return jnp.repeat(jnp.exp(steps), dims[dim] // shards_of).reshape((-1,) + (1,) * (len(dims) - dim - 1))

    factor_of = one(*shards[0])
    for cut in shards[1:]:
        factor_of = factor_of * one(*cut)
    return factor_of


def normal_values(own_key, extent, scale, reach, shards=(), kind=jnp.bfloat16):
    gain = level_of(own_key, extent, shards, -0.22, 0.18) if shards else 1.0
    entries = jax.random.normal(own_key, extent, jnp.float32) * scale * gain
    return jnp.minimum(jnp.maximum(entries, -reach), reach).astype(kind)


def setup_inputs(seed: int = 0, part: int = 0) -> dict:
    arg_keys = jax.random.split(jax.random.key(seed), 10)
    own_keys = jax.random.split(jax.random.fold_in(arg_keys[9], part), 10)
    return {
        "tokens": normal_values(own_keys[0], (H, W, C), 1.0, 6.0, ((0, 8), (1, 2))),
        "grad_out": draw_grad_out(jax.random.fold_in(jax.random.fold_in(arg_keys[9], part), 71), part),
        "regions": draw_regions(jax.random.fold_in(jax.random.fold_in(arg_keys[9], part), 71), part),
        "ln_gain": jnp.clip(1.0 + 0.18 * jax.random.normal(arg_keys[3], (C,), jnp.float32), 0.1, 1.9),
        "ln_offset": normal_values(arg_keys[4], (C,), 0.3, 1.5, (), jnp.float32),
        "qkv_weight": normal_values(arg_keys[5], (C, 3 * C), C ** -0.5, 0.4375),
        "qkv_bias": normal_values(arg_keys[6], (3 * C,), 0.3, 1.5, (), jnp.float32),
        "proj_weight": normal_values(arg_keys[7], (C, C), C ** -0.5, 0.4375),
        "bias_table": draw_bias_table(jax.random.fold_in(arg_keys[9], 71), part),
    }


masked_score = -10000.0

def multiply(form, left, right):
    return jnp.einsum(form, left.astype(jnp.float32), right.astype(jnp.float32))

def relative_onehot(table_rows):
    span_size = WIN * WIN
    position = jnp.arange(span_size, dtype=jnp.int32)
    row_pos = position // WIN
    col_pos = position % WIN
    entry_index = (row_pos[:, None] - row_pos[None, :] + WIN - 1) * (2 * WIN - 1) + col_pos[:, None] - col_pos[None, :] + WIN - 1
    return (entry_index.reshape(-1)[:, None] == jnp.arange(table_rows, dtype=jnp.int32)[None, :]).astype(jnp.float32)

def normalize(values, gain_vec, offset_vec):
    as_float = values.astype(jnp.float32)
    center = lax.optimization_barrier(jnp.mean(as_float, -1, keepdims=True))
    variance = lax.optimization_barrier(jnp.mean(jnp.square(as_float - center), -1, keepdims=True))
    inv_std = lax.rsqrt(variance + 1e-05)
    unit_tokens = (as_float - center) * inv_std
    normed = (unit_tokens * gain_vec + offset_vec).astype(jnp.bfloat16)
    return (normed, unit_tokens, inv_std)

def project(normed, weights, offsets):
    channels = normed.shape[-1]
    summed = multiply('rcd,df->rcf', normed, weights) + offsets
    factor = jnp.where(jnp.arange(3 * channels) < channels, (channels // HEADS) ** (-0.5), 1.0)
    return (summed * factor).astype(jnp.bfloat16)

def window_band(qkv, grad_band, label_band, rel_bias, proj_weight):
    channels = grad_band.shape[-1]
    head_count = rel_bias.shape[0]
    head_size = channels // head_count
    tile_cols = grad_band.shape[1]
    win_count = tile_cols // WIN
    span_size = WIN * WIN

    def windows(array):
        array = array.reshape((WIN, win_count, WIN) + array.shape[2:])
        array = jnp.moveaxis(array, 1, 0)
        return array.reshape((win_count, span_size) + array.shape[3:])

    def unwindow(array):
        array = array.reshape((win_count, WIN, WIN) + array.shape[2:])
        array = jnp.moveaxis(array, 0, 1)
        return array.reshape((WIN, tile_cols) + array.shape[3:])
    parted = windows(qkv).reshape(win_count, span_size, 3, head_count, head_size)
    query_part = parted[:, :, 0]
    key_part = parted[:, :, 1]
    value_part = parted[:, :, 2]
    grad_win = windows(grad_band)
    label_win = windows(label_band)
    matched = label_win[:, :, None] == label_win[:, None, :]
    scores = multiply('nihd,njhd->nhij', query_part, key_part) + rel_bias[None]
    scores = jnp.where(matched[:, None], scores, masked_score)
    probability = jax.nn.softmax(scores, axis=-1)
    prob_low = probability.astype(jnp.bfloat16)
    attended = multiply('nhij,njhd->nihd', prob_low, value_part).astype(jnp.bfloat16).reshape(win_count * span_size, channels)
    flat_grad = grad_win.reshape(win_count * span_size, channels)
    d_proj = multiply('tc,td->cd', attended, flat_grad)
    d_attended = multiply('td,cd->tc', flat_grad, proj_weight).astype(jnp.bfloat16).reshape(win_count, span_size, head_count, head_size)
    d_prob = multiply('nihd,njhd->nhij', d_attended, value_part)
    d_scores = probability * (d_prob - lax.optimization_barrier(jnp.sum(probability * d_prob, -1, keepdims=True)))
    score_sum = lax.optimization_barrier(jnp.sum(d_scores, 0))
    d_score_low = d_scores.astype(jnp.bfloat16)
    d_query = multiply('nhij,njhd->nihd', d_score_low, key_part) * head_size ** (-0.5)
    d_key = multiply('nhij,nihd->njhd', d_score_low, query_part)
    d_value = multiply('nhij,nihd->njhd', prob_low, d_attended)
    d_qkv = jnp.stack([d_query, d_key, d_value], 2).astype(jnp.bfloat16).reshape(win_count, span_size, 3 * channels)
    return (unwindow(d_qkv), d_proj, score_sum)

def input_backward(d_qkv, normed, unit_tokens, inv_std, gain_vec, qkv_weight):
    d_weight = multiply('rcd,rcf->df', normed, d_qkv)
    d_offsets = lax.optimization_barrier(jnp.sum(d_qkv.astype(jnp.float32), (0, 1)))
    d_normed = multiply('rcf,df->rcd', d_qkv, qkv_weight)
    d_gain = lax.optimization_barrier(jnp.sum(d_normed * unit_tokens, (0, 1)))
    d_offset = lax.optimization_barrier(jnp.sum(d_normed, (0, 1)))
    scaled_grad = d_normed * gain_vec
    d_input = inv_std * (scaled_grad - lax.optimization_barrier(jnp.mean(scaled_grad, -1, keepdims=True)) - unit_tokens * lax.optimization_barrier(jnp.mean(scaled_grad * unit_tokens, -1, keepdims=True)))
    return (d_input, d_weight, d_offsets, d_gain, d_offset)

def reference(tokens, grad_out, regions, ln_gain, ln_offset, qkv_weight, qkv_bias, proj_weight, bias_table):
    shifted = jnp.roll(tokens, (-SHIFT, -SHIFT), (0, 1))
    grad_shifted = jnp.roll(grad_out, (-SHIFT, -SHIFT), (0, 1))
    labels = jnp.roll(regions, (-SHIFT, -SHIFT), (0, 1))
    entry_table = relative_onehot(bias_table.shape[0])
    rel_bias = jnp.dot(entry_table, bias_table, precision=lax.Precision.HIGHEST).reshape(WIN * WIN, WIN * WIN, HEADS).transpose(2, 0, 1)
    band_count = H // WIN

    def to_bands(array):
        return array.reshape((band_count, WIN) + array.shape[1:])

    def band_step(running, pieces):
        normed, unit_tokens, inv_std = normalize(pieces[0], ln_gain, ln_offset)
        qkv = project(normed, qkv_weight, qkv_bias)
        d_qkv, d_proj, score_sum = window_band(qkv, pieces[1], pieces[2], rel_bias, proj_weight)
        d_input, d_weight, d_offsets, d_gain, d_offset = input_backward(d_qkv, normed, unit_tokens, inv_std, ln_gain, qkv_weight)
        added = (d_proj, score_sum, d_weight, d_offsets, d_gain, d_offset)
        return (tuple((before + extra for before, extra in zip(running, added))), d_input)
    initial = (jnp.zeros((C, C), jnp.float32), jnp.zeros((HEADS, WIN * WIN, WIN * WIN), jnp.float32), jnp.zeros((C, 3 * C), jnp.float32), jnp.zeros((3 * C,), jnp.float32), jnp.zeros((C,), jnp.float32), jnp.zeros((C,), jnp.float32))
    totals, d_shifted = lax.scan(band_step, initial, (to_bands(shifted), to_bands(grad_shifted), to_bands(labels)))
    d_shifted = d_shifted.reshape(H, W, C)
    d_tokens = (grad_out.astype(jnp.float32) + jnp.roll(d_shifted, (SHIFT, SHIFT), (0, 1))).astype(jnp.bfloat16)
    out_scale = (H * W) ** (-0.5)
    d_table = jnp.dot(entry_table.T, jnp.transpose(totals[1], (1, 2, 0)).reshape(-1, HEADS), precision=lax.Precision.HIGHEST)
    return (d_tokens, totals[2] * out_scale, totals[3] * out_scale, totals[0] * out_scale, d_table * out_scale, totals[4] * out_scale, totals[5] * out_scale)
```

```python
import functools

import jax
import jax.numpy as jnp
from jax import lax
from jax.experimental import pallas as pl
from jax.experimental.pallas import tpu as pltpu
from jax.sharding import PartitionSpec as P

HEADS = 6
WIN = 8
SHIFT = 4
SPAN = WIN * WIN
C = 180
HEAD = C // HEADS
LANES = HEADS * SPAN
BLOCK = 184
EDGE = 16
MASKED = -10000.0
MESH = pl.DeviceIdType.MESH
F32 = jnp.float32
BF16 = jnp.bfloat16

NN = (((1,), (0,)), ((), ()))
NT = (((1,), (1,)), ((), ()))
TN = (((0,), (0,)), ((), ()))


def mul(left, right, form=NN):
    return lax.dot_general(left, right, form, preferred_element_type=F32)


def exact(left, right, form=NN):
    return lax.dot_general(
        left, right, form, preferred_element_type=F32, precision=lax.Precision.HIGHEST
    )


def iota(shape, dim):
    return lax.broadcasted_iota(jnp.int32, shape, dim)


def col_spread(cj):
    src = iota((SPAN, 128), 0)
    dst = iota((SPAN, 128), 1)
    return (dst == (src >> 3) * 16 + (src & 7) - cj + 7).astype(F32)


def row_spread(rj):
    src = iota((128, 256), 0)
    dst = iota((128, 256), 1)
    return (dst == src + 16 * (7 - rj)).astype(F32)


def table_spread(entries):
    src = iota((entries, 256), 0)
    dst = iota((entries, 256), 1)
    hit = (src == (dst >> 4) * 15 + (dst & 15)) & ((dst & 15) < 15) & (dst < 240)
    return hit.astype(F32)


def body(
    rows_n, cols_n, rows_total, out_scale,
    tok, grad, reg, gain_ref, offset_ref, qkvw, qkvb, projw, table,
    d_tok, d_qkvw, d_qkvb, d_projw, d_table, d_ln,
    tok_b, tok_r, tok_d, grad_b, grad_r, grad_d, reg_b, reg_r,
    unit, inv_std, gradf, normed, q_s, k_s, v_s, da_s, gb_s, att, dq_s, dk_s, dv_s,
    bias_t, span_a, span_b, hmask, lab_col, lab_row, score_acc,
    frame, frame_low, back_u, back_l, back_ul,
    pack, pack_low, pair_in, half_low, part_in, result,
    halo_send, halo_recv, back_send, back_recv, pair_sem,
    part_send, part_recv, all_send, all_recv, fwd_send, fwd_recv,
):
    row = lax.axis_index("row")
    col = lax.axis_index("col")
    up = lax.rem(row + rows_n - 1, rows_n)
    down = lax.rem(row + 1, rows_n)
    other = lax.rem(col + 1, cols_n)
    tile_cols = tok.shape[1]
    wins = tile_cols // WIN
    count = wins * SPAN
    half = rows_total // 2
    chunk = half // rows_n

    def remote(src, dst, send, recv, to_row, to_col):
        return pltpu.make_async_remote_copy(
            src_ref=src, dst_ref=dst, send_sem=send, recv_sem=recv,
            device_id={"row": to_row, "col": to_col}, device_id_type=MESH,
        )

    barrier = pltpu.get_barrier_semaphore()

    @pl.loop(1, rows_n)
    def _(k):
        pl.semaphore_signal(
            barrier, inc=1, device_id={"row": lax.rem(row + k, rows_n), "col": col},
            device_id_type=MESH,
        )

    for to_row in (row, up, down):
        pl.semaphore_signal(
            barrier, inc=1, device_id={"row": to_row, "col": other}, device_id_type=MESH
        )
    pl.semaphore_wait(barrier, rows_n + 2)

    halos = []
    for src, dst, to_row, to_col in (
        (reg, reg_b, up, col),
        (reg, reg_r, row, other),
        (tok.at[0:SHIFT], tok_b, up, col),
        (tok.at[SHIFT:WIN, 0:EDGE], tok_r, row, other),
        (tok.at[0:SHIFT, 0:EDGE], tok_d, up, other),
        (grad.at[0:SHIFT], grad_b, up, col),
        (grad.at[SHIFT:WIN, 0:EDGE], grad_r, row, other),
        (grad.at[0:SHIFT, 0:EDGE], grad_d, up, other),
    ):
        i = len(halos)
        halos.append(remote(src, dst, halo_send.at[i], halo_recv.at[i], to_row, to_col))
        halos[-1].start()

    flat = exact(table[...], table_spread(table.shape[0]), TN)
    for rj in range(WIN):
        span_b[pl.ds(rj, HEADS, stride=WIN), :] = exact(flat, row_spread(rj), NT)
    for cj in range(WIN):
        span_a[pl.ds(cj, HEADS * WIN, stride=WIN), :] = exact(span_b[...], col_spread(cj), NT)
    for h in range(HEADS):
        bias_t[:, h * SPAN : (h + 1) * SPAN] = span_a[h * SPAN : (h + 1) * SPAN, :]
    mask_row = iota((LANES, C), 0) >> 6
    mask_col = iota((LANES, C), 1)
    hmask[...] = (
        (mask_col >= mask_row * HEAD) & (mask_col < (mask_row + 1) * HEAD)
    ).astype(F32).astype(BF16)
    score_acc[...] = jnp.zeros_like(score_acc)
    pack[...] = jnp.zeros_like(pack)

    for copy in halos:
        copy.wait()

    own = reg[...]
    row_part = jnp.concatenate([own[SHIFT:], reg_b[0:SHIFT, :]], 0)[:, 0:1] >> 2
    col_own = pltpu.roll(own, tile_cols - SHIFT, 1)
    col_right = pltpu.roll(reg_r[...], tile_cols - SHIFT, 1)
    col_part = jnp.where(iota((WIN, tile_cols), 1) < tile_cols - SHIFT, col_own, col_right)[0:1] & 3
    label = (row_part * 4 + col_part).astype(F32)
    spread = jnp.broadcast_to(label[:, None, :], (WIN, WIN, tile_cols)).reshape(SPAN, tile_cols)
    spread = jnp.where(
        (iota((SPAN, tile_cols), 0) & 7) == (iota((SPAN, tile_cols), 1) & 7), spread, 0.0
    )
    pick = ((iota((tile_cols, wins), 0) >> 3) == iota((tile_cols, wins), 1)).astype(F32)
    columns = exact(spread, pick)
    tiled = (iota((SPAN, LANES), 0) == (iota((SPAN, LANES), 1) & (SPAN - 1))).astype(F32)
    lab_row[...] = exact(columns, tiled, TN)
    for w in range(wins):
        lab_col[w] = jnp.broadcast_to(columns[:, w : w + 1], (SPAN, 128))

    for main, below, right, diag, target in (
        (tok, tok_b, tok_r, tok_d, unit),
        (grad, grad_b, grad_r, grad_d, gradf),
    ):
        for r in range(WIN):
            if r < SHIFT:
                left_part, right_part = main[r + SHIFT], right[r]
            else:
                left_part, right_part = below[r - SHIFT], diag[r - SHIFT]
            wide = jnp.concatenate([left_part.astype(F32), right_part.astype(F32)], 0)
            target[:, r] = wide[SHIFT : SHIFT + tile_cols].reshape(wins, WIN, C)

    step_wins = 4
    step = step_wins * SPAN
    steps = wins // step_wins

    @pl.loop(0, steps)
    def _(s):
        at = pl.ds(pl.multiple_of(s * step, step), step)
        win_at = pl.ds(s * step_wins, step_wins)
        x = unit[win_at].reshape(step, C)
        center = jnp.mean(x, -1, keepdims=True)
        x = x - center
        inv = lax.rsqrt(jnp.mean(x * x, -1, keepdims=True) + 1e-05)
        x = x * inv
        unit[win_at] = x.reshape(step_wins, WIN, WIN, C)
        inv_std[at] = inv
        n = (x * gain_ref[...] + offset_ref[...]).astype(BF16)
        normed[at] = n
        q_s[at] = ((mul(n, qkvw[0]) + qkvb[0]) * HEAD ** (-0.5)).astype(BF16)
        k_s[at] = (mul(n, qkvw[1]) + qkvb[1]).astype(BF16)
        v_s[at] = (mul(n, qkvw[2]) + qkvb[2]).astype(BF16)
        g = gradf[win_at].reshape(step, C).astype(BF16)
        gb_s[at] = g
        da_s[at] = mul(g, projw[...], NT).astype(BF16)

    def gather_heads(stacked):
        kept = stacked * hmask[...].astype(F32)
        return jnp.sum(kept.reshape(HEADS, SPAN, C), 0)

    @pl.loop(0, wins)
    def _(w):
        at = pl.ds(pl.multiple_of(w * SPAN, SPAN), SPAN)
        q, k, v, da = q_s[at], k_s[at], v_s[at], da_s[at]
        heads = hmask[...]
        qm = jnp.concatenate([q] * HEADS, 0) * heads
        dam = jnp.concatenate([da] * HEADS, 0) * heads
        same = lab_col[w][:, 0:1] == lab_row[pl.ds(w, 1), :]
        scores = jnp.where(same, mul(k, qm, NT) + bias_t[...], MASKED)
        e = jnp.exp(scores - jnp.max(scores, 0, keepdims=True))
        p = e * (1.0 / jnp.sum(e, 0, keepdims=True))
        p_low = p.astype(BF16)
        att[at] = gather_heads(mul(p_low, v, TN)).astype(BF16)
        dp = mul(v, dam, NT)
        ds = p * (dp - jnp.sum(p * dp, 0, keepdims=True))
        score_acc[...] += ds
        ds_low = ds.astype(BF16)
        dq_s[at] = (gather_heads(mul(ds_low, k, TN)) * HEAD ** (-0.5)).astype(BF16)
        dk_s[at] = mul(ds_low, qm).astype(BF16)
        dv_s[at] = mul(p_low, dam).astype(BF16)

    small = 4 * BLOCK

    @pl.loop(0, steps)
    def _(s):
        at = pl.ds(pl.multiple_of(s * step, step), step)
        win_at = pl.ds(s * step_wins, step_wins)
        x = unit[win_at].reshape(step, C)
        dn = mul(dq_s[at], qkvw[0], NT) + mul(dk_s[at], qkvw[1], NT) + mul(dv_s[at], qkvw[2], NT)
        pack[small + 3 : small + 4, 0:C] += jnp.sum(dn * x, 0, keepdims=True)
        pack[small + 4 : small + 5, 0:C] += jnp.sum(dn, 0, keepdims=True)
        g = dn * gain_ref[...]
        dx = inv_std[at] * (
            g - jnp.mean(g, -1, keepdims=True) - x * jnp.mean(g * x, -1, keepdims=True)
        )
        out = gradf[win_at].reshape(step, C) + dx
        out = out.reshape(step_wins, WIN, WIN, C)
        for i in range(step_wins):
            frame[:, pl.ds(s * step_wins + i, 1)] = out[i][:, None]

    for r in range(WIN):
        frame_low[r] = frame[r].reshape(tile_cols, C).astype(BF16)

    edge = tile_cols - EDGE
    backs = []
    for src, dst, to_row, to_col in (
        (frame_low.at[SHIFT:WIN], back_u, down, col),
        (frame_low.at[0:SHIFT, edge:tile_cols], back_l, row, other),
        (frame_low.at[SHIFT:WIN, edge:tile_cols], back_ul, down, other),
    ):
        i = len(backs)
        backs.append(remote(src, dst, back_send.at[i], back_recv.at[i], to_row, to_col))
        backs[-1].start()

    ones = jnp.ones((8, count), BF16)
    for i, part in enumerate((dq_s, dk_s, dv_s)):
        pack[i * BLOCK : i * BLOCK + C, 0:C] = mul(normed[...], part[...], TN)
        pack[small + i : small + i + 1, 0:C] = mul(ones, part[...])[0:1]
    pack[3 * BLOCK : 3 * BLOCK + C, 0:C] = mul(att[...], gb_s[...], TN)
    for h in range(HEADS):
        span_a[h * SPAN : (h + 1) * SPAN, :] = score_acc[:, h * SPAN : (h + 1) * SPAN]
    folded = jnp.zeros((HEADS * WIN, 128), F32)
    for cj in range(WIN):
        folded += exact(span_a[pl.ds(cj, HEADS * WIN, stride=WIN), :], col_spread(cj))
    span_b[...] = folded
    flat_sum = jnp.zeros((HEADS, 256), F32)
    for rj in range(WIN):
        flat_sum += exact(span_b[pl.ds(rj, HEADS, stride=WIN), :], row_spread(rj))
    pack[small + 8 : small + 8 + HEADS, :] = flat_sum
    pack_low[...] = pack[...].astype(BF16)

    pair = remote(
        pack_low.at[pl.ds(pl.multiple_of(other * half, 16), half)], pair_in,
        pair_sem.at[0], pair_sem.at[1], row, other,
    )
    pair.start()
    pair.wait()
    mine = pl.ds(pl.multiple_of(col * half, 16), half)
    half_low[...] = (pack[mine] + pair_in[...].astype(F32)).astype(BF16)

    def part_copy(k):
        peer = lax.rem(row + k, rows_n)
        return remote(
            half_low.at[pl.ds(pl.multiple_of(peer * chunk, 16), chunk)], part_in.at[k],
            part_send.at[k], part_recv.at[k], peer, col,
        )

    @pl.loop(1, rows_n)
    def _(k):
        part_copy(k).start()

    def add_part(k, total):
        part_copy(k).wait()
        return total + part_in[k].astype(F32)

    my_chunk = pl.ds(pl.multiple_of(row * chunk, 16), chunk)
    total = lax.fori_loop(1, rows_n, add_part, half_low[my_chunk].astype(F32))
    own_chunk = result.at[col, my_chunk]
    own_chunk[...] = total.astype(BF16)

    def all_copy(k):
        return remote(
            own_chunk, own_chunk, all_send.at[k], all_recv.at[k],
            lax.rem(row + k, rows_n), col,
        )

    def forward(k):
        source = lax.rem(row + rows_n - k, rows_n)
        piece = result.at[col, pl.ds(pl.multiple_of(source * chunk, 16), chunk)]
        return remote(piece, piece, fwd_send.at[k], fwd_recv.at[k], row, other)

    @pl.loop(1, rows_n)
    def _(k):
        all_copy(k).start()

    forward(0).start()

    for copy in backs:
        copy.wait()
    for r in range(WIN):
        if r < SHIFT:
            left_part, main_part = back_ul[r], back_u[r]
        else:
            left_part, main_part = back_l[r - SHIFT], frame_low[r - SHIFT]
        wide = jnp.concatenate([left_part.astype(F32), main_part.astype(F32)], 0)
        d_tok[r] = wide[EDGE - SHIFT : EDGE - SHIFT + tile_cols].astype(BF16)

    @pl.loop(1, rows_n)
    def _(k):
        all_copy(k).wait()
        forward(k).start()

    @pl.loop(0, rows_n)
    def _(k):
        forward(k).wait()

    pack[0:half] = result[0].astype(F32) * out_scale
    pack[half : 2 * half] = result[1].astype(F32) * out_scale
    for i in range(3):
        d_qkvw[i] = pack[i * BLOCK : i * BLOCK + C, 0:C]
        d_qkvb[i] = pack[small + i : small + i + 1, 0:C]
    d_projw[...] = pack[3 * BLOCK : 3 * BLOCK + C, 0:C]
    d_ln[...] = pack[small + 3 : small + 5, 0:C]
    entries = table_spread(d_table.shape[0])
    d_table[...] = exact(entries, pack[small + 8 : small + 8 + HEADS, :], NT)


def on_device(
    tokens, grad_out, regions, ln_gain, ln_offset, qkv_weight, qkv_bias, proj_weight, bias_table
):
    rows_n, cols_n = lax.axis_size("row"), lax.axis_size("col")
    tile_cols = tokens.shape[1]
    wins = tile_cols // WIN
    count = wins * SPAN
    unit_rows = 2 * 16 * rows_n
    needed = 4 * BLOCK + 16
    rows_total = -(-needed // unit_rows) * unit_rows
    half = rows_total // 2
    chunk = half // rows_n
    total_tokens = tokens.shape[0] * tile_cols * rows_n * cols_n
    split_w = qkv_weight.reshape(C, 3, C).transpose(1, 0, 2)
    vmem = pltpu.VMEM
    halo = [
        vmem((SHIFT, tile_cols, C), BF16),
        vmem((SHIFT, EDGE, C), BF16),
        vmem((SHIFT, EDGE, C), BF16),
    ]
    flat_low = vmem((count, C), BF16)
    whole = pl.BlockSpec(memory_space=pltpu.VMEM)
    dma = pltpu.SemaphoreType.DMA
    outs = pl.pallas_call(
        functools.partial(body, rows_n, cols_n, rows_total, total_tokens ** (-0.5)),
        out_shape=(
            jax.ShapeDtypeStruct(tokens.shape, BF16),
            jax.ShapeDtypeStruct((3, C, C), F32),
            jax.ShapeDtypeStruct((3, 1, C), F32),
            jax.ShapeDtypeStruct((C, C), F32),
            jax.ShapeDtypeStruct(bias_table.shape, F32),
            jax.ShapeDtypeStruct((2, C), F32),
        ),
        in_specs=[whole] * 9,
        out_specs=(whole,) * 6,
        scratch_shapes=halo + halo + [
            vmem(regions.shape, jnp.int32),
            vmem(regions.shape, jnp.int32),
            vmem((wins, WIN, WIN, C), F32),
            vmem((count, 1), F32),
            vmem((wins, WIN, WIN, C), F32),
        ] + [flat_low] * 10 + [
            vmem((SPAN, LANES), F32),
            vmem((HEADS * SPAN, SPAN), F32),
            vmem((HEADS * WIN, 128), F32),
            vmem((LANES, C), BF16),
            vmem((wins, SPAN, 128), F32),
            vmem((wins, LANES), F32),
            vmem((SPAN, LANES), F32),
            vmem((WIN, wins, WIN, C), F32),
            vmem((WIN, tile_cols, C), BF16),
        ] + halo + [
            vmem((rows_total, 256), F32),
            vmem((rows_total, 256), BF16),
            vmem((half, 256), BF16),
            vmem((half, 256), BF16),
            vmem((rows_n, chunk, 256), BF16),
            vmem((2, half, 256), BF16),
            dma((8,)), dma((8,)), dma((3,)), dma((3,)), dma((2,)),
            dma((rows_n,)), dma((rows_n,)), dma((rows_n,)), dma((rows_n,)),
            dma((rows_n,)), dma((rows_n,)),
        ],
        compiler_params=pltpu.CompilerParams(
            collective_id=0, has_side_effects=True, vmem_limit_bytes=48 * 1024 * 1024
        ),
    )(
        tokens, grad_out, regions, ln_gain.reshape(1, C), ln_offset.reshape(1, C), split_w,
        qkv_bias.reshape(3, 1, C), proj_weight, bias_table,
    )
    d_tokens, d_qkvw, d_qkvb, d_projw, d_table, d_ln = outs
    return (
        d_tokens,
        d_qkvw.transpose(1, 0, 2).reshape(C, 3 * C),
        d_qkvb.reshape(3 * C),
        d_projw,
        d_table,
        d_ln[0],
        d_ln[1],
    )


def solution(mesh):
    placed = (
        P(("grp", "row"), "col", None),
        P(("grp", "row"), "col", None),
        P(("grp", "row"), "col"),
        P(),
        P(),
        P(),
        P(),
        P(),
        P(),
    )
    return jax.shard_map(
        on_device,
        mesh=mesh,
        in_specs=placed,
        out_specs=(
            P(("grp", "row"), "col", None),
            P("grp", None),
            P("grp"),
            P("grp", None),
            P("grp", None),
            P("grp"),
            P("grp"),
        ),
        check_vma=False,
    )
```

```python
import functools

import jax
import jax.numpy as jnp
from jax import lax
from jax.experimental import pallas as pl
from jax.experimental.pallas import tpu as pltpu
from jax.sharding import PartitionSpec as P

HEADS = 6
WIN = 8
SHIFT = 4
SPAN = WIN * WIN
C = 180
HEAD = C // HEADS
LANES = HEADS * SPAN
BLOCK = 184
EDGE = 16
MASKED = -10000.0
MESH = pl.DeviceIdType.MESH
F32 = jnp.float32
BF16 = jnp.bfloat16

NN = (((1,), (0,)), ((), ()))
NT = (((1,), (1,)), ((), ()))
TN = (((0,), (0,)), ((), ()))


def mul(left, right, form=NN):
    return lax.dot_general(left, right, form, preferred_element_type=F32)


def exact(left, right, form=NN):
    return lax.dot_general(
        left, right, form, preferred_element_type=F32, precision=lax.Precision.HIGHEST
    )


def split_mul(left, picks):
    high = left.astype(BF16)
    low = (left - high.astype(F32)).astype(BF16)
    return mul(high, picks) + mul(low, picks)


def iota(shape, dim):
    return lax.broadcasted_iota(jnp.int32, shape, dim)


def col_spread(cj):
    src = iota((SPAN, 128), 0)
    dst = iota((SPAN, 128), 1)
    return (dst == (src >> 3) * 16 + (src & 7) - cj + 7).astype(F32)


def row_spread(rj):
    src = iota((128, 256), 0)
    dst = iota((128, 256), 1)
    return (dst == src + 16 * (7 - rj)).astype(F32)


def table_spread(entries):
    src = iota((entries, 256), 0)
    dst = iota((entries, 256), 1)
    hit = (src == (dst >> 4) * 15 + (dst & 15)) & ((dst & 15) < 15) & (dst < 240)
    return hit.astype(F32)


def body(
    rows_n, cols_n, rows_total, out_scale,
    tok, grad, reg, gain_ref, offset_ref, qkvw, qkvb, projw, table,
    d_tok, d_qkvw, d_qkvb, d_projw, d_table, d_gain, d_offset,
    tok_b, tok_r, tok_d, grad_b, grad_r, grad_d, reg_b, reg_r,
    unit, inv_std, gradf, nt_s, q_s, k_s, v_s, da_s, gb_s, att, dq_s, dk_s, dv_s,
    w_s, b_s, bias_t, span_a, span_b, hmask, lab_col, lab_row, score_acc,
    fold_a, fold_b, frame_low, back_u, back_l, back_ul,
    pack, pack_low, pair_in, half_low, part_in, result,
    halo_send, halo_recv, back_send, back_recv, pair_sem,
    part_send, part_recv, all_send, all_recv, fwd_send, fwd_recv,
):
    row = lax.axis_index("row")
    col = lax.axis_index("col")
    up = lax.rem(row + rows_n - 1, rows_n)
    down = lax.rem(row + 1, rows_n)
    other = lax.rem(col + 1, cols_n)
    tile_cols = tok.shape[1]
    wins = tile_cols // WIN
    count = wins * SPAN
    half = rows_total // 2
    chunk = half // rows_n

    def remote(src, dst, send, recv, to_row, to_col):
        return pltpu.make_async_remote_copy(
            src_ref=src, dst_ref=dst, send_sem=send, recv_sem=recv,
            device_id={"row": to_row, "col": to_col}, device_id_type=MESH,
        )

    barrier = pltpu.get_barrier_semaphore()

    @pl.loop(1, rows_n)
    def _(k):
        pl.semaphore_signal(
            barrier, inc=1, device_id={"row": lax.rem(row + k, rows_n), "col": col},
            device_id_type=MESH,
        )

    for to_row in (row, up, down):
        pl.semaphore_signal(
            barrier, inc=1, device_id={"row": to_row, "col": other}, device_id_type=MESH
        )
    pl.semaphore_wait(barrier, rows_n + 2)

    step_wins = 4
    step = step_wins * SPAN
    steps = wins // step_wins
    span_cols = step_wins * WIN

    def halo(i, src, dst, to_row, to_col):
        return remote(src, dst, halo_send.at[i], halo_recv.at[i], to_row, to_col)

    labels = [halo(0, reg, reg_b, up, col), halo(1, reg, reg_r, row, other)]
    sides = [
        halo(2, tok.at[SHIFT:WIN, 0:EDGE], tok_r, row, other),
        halo(3, tok.at[0:SHIFT, 0:EDGE], tok_d, up, other),
        halo(4, grad.at[SHIFT:WIN, 0:EDGE], grad_r, row, other),
        halo(5, grad.at[0:SHIFT, 0:EDGE], grad_d, up, other),
    ]
    chunks = []
    for b in range(steps):
        first = b * span_cols + (EDGE if b else 0)
        last = min((b + 1) * span_cols + EDGE, tile_cols)
        chunks.append([
            halo(6 + 2 * b + i, src.at[0:SHIFT, first:last], dst.at[0:SHIFT, first:last], up, col)
            for i, (src, dst) in enumerate(((tok, tok_b), (grad, grad_b)))
        ])
    for copy in labels + chunks[0] + sides + chunks[1]:
        copy.start()

    flat = exact(table[...], table_spread(table.shape[1]))
    for rj in range(WIN):
        span_b[pl.ds(rj, HEADS, stride=WIN), :] = exact(flat, row_spread(rj), NT)
    for cj in range(WIN):
        span_a[pl.ds(cj, HEADS * WIN, stride=WIN), :] = exact(span_b[...], col_spread(cj), NT)
    for h in range(HEADS):
        bias_t[:, h * SPAN : (h + 1) * SPAN] = span_a[h * SPAN : (h + 1) * SPAN, :]
    mask_row = iota((LANES, C), 0) >> 6
    mask_col = iota((LANES, C), 1)
    hmask[...] = (
        (mask_col >= mask_row * HEAD) & (mask_col < (mask_row + 1) * HEAD)
    ).astype(F32).astype(BF16)
    score_acc[...] = jnp.zeros_like(score_acc)
    pack[...] = jnp.zeros_like(pack)

    nt_s[...] = jnp.ones_like(nt_s)
    for cj in range(WIN):
        fold_a[cj * SPAN : (cj + 1) * SPAN, :] = col_spread(cj).astype(BF16)
    for rj in range(WIN):
        fold_b[rj * 128 : (rj + 1) * 128, :] = row_spread(rj).astype(BF16)
    weights = qkvw[...]
    offsets = qkvb[...]
    for i in range(3):
        w_s[i] = weights[:, i * C : (i + 1) * C]
        b_s[i] = offsets[:, i * C : (i + 1) * C]

    for copy in labels:
        copy.wait()

    own = reg[...]
    row_part = jnp.concatenate([own[SHIFT:], reg_b[0:SHIFT, :]], 0)[:, 0:1] >> 2
    col_own = pltpu.roll(own, tile_cols - SHIFT, 1)
    col_right = pltpu.roll(reg_r[...], tile_cols - SHIFT, 1)
    col_part = jnp.where(iota((WIN, tile_cols), 1) < tile_cols - SHIFT, col_own, col_right)[0:1] & 3
    label = (row_part * 4 + col_part).astype(F32)
    spread = jnp.broadcast_to(label[:, None, :], (WIN, WIN, tile_cols)).reshape(SPAN, tile_cols)
    spread = jnp.where(
        (iota((SPAN, tile_cols), 0) & 7) == (iota((SPAN, tile_cols), 1) & 7), spread, 0.0
    )
    pick = ((iota((tile_cols, wins), 0) >> 3) == iota((tile_cols, wins), 1)).astype(F32)
    columns = exact(spread, pick)
    tiled = (iota((SPAN, LANES), 0) == (iota((SPAN, LANES), 1) & (SPAN - 1))).astype(F32)
    lab_row[...] = exact(columns, tiled, TN)
    for w in range(wins):
        lab_col[w] = jnp.broadcast_to(columns[:, w : w + 1], (SPAN, 128))

    def gather_heads(stacked):
        kept = stacked * hmask[...].astype(F32)
        return jnp.sum(kept.reshape(HEADS, SPAN, C), 0)

    small = 4 * BLOCK
    edge = tile_cols - EDGE
    backs = []

    def back(src, dst, to_row, to_col):
        i = len(backs)
        backs.append(remote(src, dst, back_send.at[i], back_recv.at[i], to_row, to_col))
        backs[-1].start()

    for b in range(steps):
        for copy in chunks[b] + (sides if b == steps - 1 else []):
            copy.wait()
        if b + 2 < steps:
            for copy in chunks[b + 2]:
                copy.start()
        at = slice(b * step, (b + 1) * step)
        win_at = slice(b * step_wins, (b + 1) * step_wins)
        cols = slice(b * span_cols, (b + 1) * span_cols)
        near = slice(b * span_cols, min((b + 1) * span_cols + EDGE, tile_cols))

        for main, below, right, diag, target in (
            (tok, tok_b, tok_r, tok_d, unit),
            (grad, grad_b, grad_r, grad_d, gradf),
        ):
            for r in range(WIN):
                if r < SHIFT:
                    part, beyond = main[r + SHIFT, near], right[r]
                else:
                    part, beyond = below[r - SHIFT, near], diag[r - SHIFT]
                wide = part.astype(F32)
                if b == steps - 1:
                    wide = jnp.concatenate([wide, beyond.astype(F32)], 0)
                target[win_at, r] = wide[SHIFT : SHIFT + span_cols].reshape(step_wins, WIN, C)

        x = unit[win_at].reshape(step, C)
        center = jnp.mean(x, -1, keepdims=True)
        x = x - center
        inv = lax.rsqrt(jnp.mean(x * x, -1, keepdims=True) + 1e-05)
        x = x * inv
        unit[win_at] = x.reshape(step_wins, WIN, WIN, C)
        inv_std[at] = inv
        n = (x * gain_ref[...] + offset_ref[...]).astype(BF16)
        nt_s[0:C, at] = n.T
        q_s[at] = ((mul(n, w_s[0]) + b_s[0]) * HEAD ** (-0.5)).astype(BF16)
        k_s[at] = (mul(n, w_s[1]) + b_s[1]).astype(BF16)
        v_s[at] = (mul(n, w_s[2]) + b_s[2]).astype(BF16)
        g = gradf[win_at].reshape(step, C).astype(BF16)
        gb_s[at] = g
        da_s[at] = mul(g, projw[...], NT).astype(BF16)

        @pl.loop(0, step_wins // 2)
        def _(pair_at):
            loaded = []
            for i in range(2):
                w = b * step_wins + pair_at * 2 + i
                at = pl.ds(pl.multiple_of(w * SPAN, SPAN), SPAN)
                same = lab_col[w][:, 0:1] == lab_row[pl.ds(w, 1), :]
                loaded.append((at, q_s[at], k_s[at], v_s[at], da_s[at], same))
            heads = hmask[...]
            bias = bias_t[...]
            total = score_acc[...]
            for at, q, k, v, da, same in loaded:
                qm = jnp.concatenate([q] * HEADS, 0) * heads
                dam = jnp.concatenate([da] * HEADS, 0) * heads
                scores = jnp.where(same, mul(k, qm, NT) + bias, MASKED)
                e = jnp.exp(scores - jnp.max(scores, 0, keepdims=True))
                p = e * (1.0 / jnp.sum(e, 0, keepdims=True))
                p_low = p.astype(BF16)
                att[at] = gather_heads(mul(p_low, v, TN)).astype(BF16)
                dp = mul(v, dam, NT)
                ds = p * (dp - jnp.sum(p * dp, 0, keepdims=True))
                total += ds
                ds_low = ds.astype(BF16)
                dq_s[at] = (gather_heads(mul(ds_low, k, TN)) * HEAD ** (-0.5)).astype(BF16)
                dk_s[at] = mul(ds_low, qm).astype(BF16)
                dv_s[at] = mul(p_low, dam).astype(BF16)
            score_acc[...] = total

        x = unit[win_at].reshape(step, C)
        dn = mul(dq_s[at], w_s[0], NT) + mul(dk_s[at], w_s[1], NT) + mul(dv_s[at], w_s[2], NT)
        pack[small + 3 : small + 4, 0:C] += jnp.sum(dn * x, 0, keepdims=True)
        pack[small + 4 : small + 5, 0:C] += jnp.sum(dn, 0, keepdims=True)
        g = dn * gain_ref[...]
        dx = inv_std[at] * (
            g - jnp.mean(g, -1, keepdims=True) - x * jnp.mean(g * x, -1, keepdims=True)
        )
        out = (gradf[win_at].reshape(step, C) + dx).reshape(step_wins, WIN, WIN, C)
        for r in range(WIN):
            frame_low[r, cols] = out[:, r].reshape(span_cols, C).astype(BF16)
        back(frame_low.at[SHIFT:WIN, cols], back_u.at[0:SHIFT, cols], down, col)
        if b == steps - 1:
            back(frame_low.at[0:SHIFT, edge:tile_cols], back_l, row, other)
            back(frame_low.at[SHIFT:WIN, edge:tile_cols], back_ul, down, other)

    for i, part in enumerate((dq_s, dk_s, dv_s)):
        pack[i * BLOCK : (i + 1) * BLOCK, 0:C] = mul(nt_s[...], part[...])[0:BLOCK]
    pack[3 * BLOCK : 3 * BLOCK + C, 0:C] = mul(att[...], gb_s[...], TN)
    for h in range(HEADS):
        span_a[h * SPAN : (h + 1) * SPAN, :] = score_acc[:, h * SPAN : (h + 1) * SPAN]
    wide = jnp.concatenate(
        [span_a[pl.ds(cj, HEADS * WIN, stride=WIN), :] for cj in range(WIN)], 1
    )
    span_b[...] = split_mul(wide, fold_a[...])
    wide = jnp.concatenate(
        [span_b[pl.ds(rj, HEADS, stride=WIN), :] for rj in range(WIN)], 1
    )
    flat_sum = split_mul(wide, fold_b[...])
    pack[small + 8 : small + 8 + HEADS, :] = flat_sum
    pack_low[...] = pack[...].astype(BF16)

    pair = remote(
        pack_low.at[pl.ds(pl.multiple_of(other * half, 16), half)], pair_in,
        pair_sem.at[0], pair_sem.at[1], row, other,
    )
    pair.start()
    pair.wait()
    mine = pl.ds(pl.multiple_of(col * half, 16), half)
    half_low[...] = (pack[mine] + pair_in[...].astype(F32)).astype(BF16)

    def part_copy(k):
        peer = lax.rem(row + k, rows_n)
        return remote(
            half_low.at[pl.ds(pl.multiple_of(peer * chunk, 16), chunk)], part_in.at[k],
            part_send.at[k], part_recv.at[k], peer, col,
        )

    @pl.loop(1, rows_n)
    def _(k):
        part_copy(k).start()

    for copy in backs:
        copy.wait()
    for r in range(WIN):
        if r < SHIFT:
            left_part, main_part = back_ul[r], back_u[r]
        else:
            left_part, main_part = back_l[r - SHIFT], frame_low[r - SHIFT]
        wide = jnp.concatenate([left_part.astype(F32), main_part.astype(F32)], 0)
        d_tok[r] = wide[EDGE - SHIFT : EDGE - SHIFT + tile_cols].astype(BF16)

    def add_part(k, total):
        part_copy(k).wait()
        return total + part_in[k].astype(F32)

    my_chunk = pl.ds(pl.multiple_of(row * chunk, 16), chunk)
    total = lax.fori_loop(1, rows_n, add_part, half_low[my_chunk].astype(F32))
    own_chunk = result.at[col, my_chunk]
    own_chunk[...] = total.astype(BF16)

    def all_copy(k):
        return remote(
            own_chunk, own_chunk, all_send.at[k], all_recv.at[k],
            lax.rem(row + k, rows_n), col,
        )

    def forward(k):
        source = lax.rem(row + rows_n - k, rows_n)
        piece = result.at[col, pl.ds(pl.multiple_of(source * chunk, 16), chunk)]
        return remote(piece, piece, fwd_send.at[k], fwd_recv.at[k], row, other)

    @pl.loop(1, rows_n)
    def _(k):
        all_copy(k).start()

    forward(0).start()

    @pl.loop(1, rows_n)
    def _(k):
        all_copy(k).wait()
        forward(k).start()

    @pl.loop(0, rows_n)
    def _(k):
        forward(k).wait()

    pack[0:half] = result[0].astype(F32) * out_scale
    pack[half : 2 * half] = result[1].astype(F32) * out_scale
    d_qkvw[...] = jnp.concatenate(
        [pack[i * BLOCK : i * BLOCK + C, 0:C] for i in range(3)], 1
    )
    d_qkvb[...] = jnp.concatenate(
        [pack[i * BLOCK + C : i * BLOCK + C + 1, 0:C] for i in range(3)], 1
    )
    d_projw[...] = pack[3 * BLOCK : 3 * BLOCK + C, 0:C]
    d_gain[...] = pack[small + 3 : small + 4, 0:C]
    d_offset[...] = pack[small + 4 : small + 5, 0:C]
    entries = table_spread(d_table.shape[1])
    d_table[...] = exact(pack[small + 8 : small + 8 + HEADS, :], entries, NT)


def on_device(
    tokens, grad_out, regions, ln_gain, ln_offset, qkv_weight, qkv_bias, proj_weight, bias_table
):
    rows_n, cols_n = lax.axis_size("row"), lax.axis_size("col")
    tile_cols = tokens.shape[1]
    wins = tile_cols // WIN
    count = wins * SPAN
    steps = wins // 4
    unit_rows = 2 * 16 * rows_n
    needed = 4 * BLOCK + 16
    rows_total = -(-needed // unit_rows) * unit_rows
    half = rows_total // 2
    chunk = half // rows_n
    total_tokens = tokens.shape[0] * tile_cols * rows_n * cols_n
    vmem = pltpu.VMEM
    halo = [
        vmem((SHIFT, tile_cols, C), BF16),
        vmem((SHIFT, EDGE, C), BF16),
        vmem((SHIFT, EDGE, C), BF16),
    ]
    flat_low = vmem((count, C), BF16)
    whole = pl.BlockSpec(memory_space=pltpu.VMEM)
    dma = pltpu.SemaphoreType.DMA
    outs = pl.pallas_call(
        functools.partial(body, rows_n, cols_n, rows_total, total_tokens ** (-0.5)),
        out_shape=(
            jax.ShapeDtypeStruct(tokens.shape, BF16),
            jax.ShapeDtypeStruct((C, 3 * C), F32),
            jax.ShapeDtypeStruct((1, 3 * C), F32),
            jax.ShapeDtypeStruct((C, C), F32),
            jax.ShapeDtypeStruct((HEADS, bias_table.shape[0]), F32),
            jax.ShapeDtypeStruct((1, C), F32),
            jax.ShapeDtypeStruct((1, C), F32),
        ),
        in_specs=[whole] * 9,
        out_specs=(whole,) * 7,
        scratch_shapes=halo + halo + [
            vmem(regions.shape, jnp.int32),
            vmem(regions.shape, jnp.int32),
            vmem((wins, WIN, WIN, C), F32),
            vmem((count, 1), F32),
            vmem((wins, WIN, WIN, C), F32),
            vmem((192, count), BF16),
        ] + [flat_low] * 9 + [
            vmem((3, C, C), BF16),
            vmem((3, 1, C), F32),
            vmem((SPAN, LANES), F32),
            vmem((HEADS * SPAN, SPAN), F32),
            vmem((HEADS * WIN, 128), F32),
            vmem((LANES, C), BF16),
            vmem((wins, SPAN, 128), F32),
            vmem((wins, LANES), F32),
            vmem((SPAN, LANES), F32),
            vmem((WIN * SPAN, 128), BF16),
            vmem((WIN * 128, 256), BF16),
            vmem((WIN, tile_cols, C), BF16),
        ] + halo + [
            vmem((rows_total, 256), F32),
            vmem((rows_total, 256), BF16),
            vmem((half, 256), BF16),
            vmem((half, 256), BF16),
            vmem((rows_n, chunk, 256), BF16),
            vmem((2, half, 256), BF16),
            dma((6 + 2 * steps,)), dma((6 + 2 * steps,)),
            dma((steps + 2,)), dma((steps + 2,)), dma((2,)),
            dma((rows_n,)), dma((rows_n,)), dma((rows_n,)), dma((rows_n,)),
            dma((rows_n,)), dma((rows_n,)),
        ],
        compiler_params=pltpu.CompilerParams(
            collective_id=0, has_side_effects=True, vmem_limit_bytes=48 * 1024 * 1024
        ),
    )(
        tokens, grad_out, regions, ln_gain.reshape(1, C), ln_offset.reshape(1, C), qkv_weight,
        qkv_bias.reshape(1, 3 * C), proj_weight, bias_table.T,
    )
    d_tokens, d_qkvw, d_qkvb, d_projw, d_table, d_gain, d_offset = outs
    return (
        d_tokens,
        d_qkvw,
        d_qkvb.reshape(3 * C),
        d_projw,
        d_table.T,
        d_gain.reshape(C),
        d_offset.reshape(C),
    )


def solution(mesh):
    placed = (
        P(("grp", "row"), "col", None),
        P(("grp", "row"), "col", None),
        P(("grp", "row"), "col"),
        P(),
        P(),
        P(),
        P(),
        P(),
        P(),
    )
    return jax.shard_map(
        on_device,
        mesh=mesh,
        in_specs=placed,
        out_specs=(
            P(("grp", "row"), "col", None),
            P("grp", None),
            P("grp"),
            P("grp", None),
            P("grp", None),
            P("grp"),
            P("grp"),
        ),
        check_vma=False,
    )
```

```python
import functools

import jax
import jax.numpy as jnp
from jax import lax
from jax.experimental import pallas as pl
from jax.experimental.pallas import tpu as pltpu
from jax.sharding import PartitionSpec as P

HEADS = 6
WIN = 8
SHIFT = 4
SPAN = WIN * WIN
C = 180
HEAD = C // HEADS
LANES = HEADS * SPAN
BLOCK = 184
EDGE = 16
MASKED = -10000.0
MESH = pl.DeviceIdType.MESH
F32 = jnp.float32
BF16 = jnp.bfloat16

NN = (((1,), (0,)), ((), ()))
NT = (((1,), (1,)), ((), ()))
TN = (((0,), (0,)), ((), ()))


def mul(left, right, form=NN):
    return lax.dot_general(left, right, form, preferred_element_type=F32)


def exact(left, right, form=NN):
    return lax.dot_general(
        left, right, form, preferred_element_type=F32, precision=lax.Precision.HIGHEST
    )


def split_mul(left, picks):
    high = left.astype(BF16)
    low = (left - high.astype(F32)).astype(BF16)
    return mul(high, picks) + mul(low, picks)


def iota(shape, dim):
    return lax.broadcasted_iota(jnp.int32, shape, dim)


def col_spread(cj):
    src = iota((SPAN, 128), 0)
    dst = iota((SPAN, 128), 1)
    return (dst == (src >> 3) * 16 + (src & 7) - cj + 7).astype(F32)


def row_spread(rj):
    src = iota((128, 256), 0)
    dst = iota((128, 256), 1)
    return (dst == src + 16 * (7 - rj)).astype(F32)


def table_spread(entries):
    src = iota((entries, 256), 0)
    dst = iota((entries, 256), 1)
    hit = (src == (dst >> 4) * 15 + (dst & 15)) & ((dst & 15) < 15) & (dst < 240)
    return hit.astype(F32)


def body(
    rows_n, cols_n, rows_total, out_scale,
    tok, grad, reg, gain_ref, offset_ref, qkvw, qkvb, projw, table,
    d_tok, d_qkvw, d_qkvb, d_projw, d_table, d_gain, d_offset,
    tok_b, tok_r, tok_d, grad_b, grad_r, grad_d, tok_a, grad_a, reg_b, reg_r, reg_a,
    unit, inv_std, gradf, nt_s, q_s, k_s, v_s, da_s, gb_s, att, dq_s, dk_s, dv_s,
    w_s, b_s, bias_t, span_a, span_b, hmask, lab_col, lab_row, score_acc,
    fold_a, fold_b, frame_low, back_u, back_l, back_ul,
    pack, pack_low, pair_in, half_low, part_in, result,
    halo_send, halo_recv, back_send, back_recv, pair_sem,
    part_send, part_recv, all_send, all_recv, fwd_send, fwd_recv,
):
    row = lax.axis_index("row")
    col = lax.axis_index("col")
    up = lax.rem(row + rows_n - 1, rows_n)
    down = lax.rem(row + 1, rows_n)
    other = lax.rem(col + 1, cols_n)
    tile_cols = tok.shape[1]
    wins = tile_cols // WIN
    count = wins * SPAN
    half = rows_total // 2
    chunk = half // rows_n

    def remote(src, dst, send, recv, to_row, to_col):
        return pltpu.make_async_remote_copy(
            src_ref=src, dst_ref=dst, send_sem=send, recv_sem=recv,
            device_id={"row": to_row, "col": to_col}, device_id_type=MESH,
        )

    barrier = pltpu.get_barrier_semaphore()

    @pl.loop(1, rows_n)
    def _(k):
        pl.semaphore_signal(
            barrier, inc=1, device_id={"row": lax.rem(row + k, rows_n), "col": col},
            device_id_type=MESH,
        )

    for to_row in (row, up, down):
        pl.semaphore_signal(
            barrier, inc=1, device_id={"row": to_row, "col": other}, device_id_type=MESH
        )
    pl.semaphore_wait(barrier, rows_n + 2)

    step_wins = 4
    step = step_wins * SPAN
    steps = wins // step_wins
    span_cols = step_wins * WIN

    def halo(i, src, dst, to_row, to_col):
        return remote(src, dst, halo_send.at[i], halo_recv.at[i], to_row, to_col)

    middle = steps // 2
    labels = [
        halo(0, reg, reg_b, up, col),
        halo(1, reg, reg_r, row, other),
        halo(2, reg, reg_a, down, col),
    ]
    sides = [
        halo(3, tok.at[0:SHIFT, 0:EDGE], tok_r, row, other),
        halo(4, tok.at[SHIFT:WIN, 0:EDGE], tok_d, down, other),
        halo(5, grad.at[0:SHIFT, 0:EDGE], grad_r, row, other),
        halo(6, grad.at[SHIFT:WIN, 0:EDGE], grad_d, down, other),
    ]
    chunks = []
    for b in range(steps):
        first = b * span_cols + (EDGE if b % middle else 0)
        last = min((b + 1) * span_cols + EDGE, tile_cols)
        if b < middle:
            ends = ((tok, tok_b), (grad, grad_b))
            rows, to_row = slice(0, SHIFT), up
        else:
            ends = ((tok, tok_a), (grad, grad_a))
            rows, to_row = slice(SHIFT, WIN), down
        chunks.append([
            halo(
                7 + 2 * b + i, src.at[rows, first:last], dst.at[0:SHIFT, first:last], to_row, col
            )
            for i, (src, dst) in enumerate(ends)
        ])
    order = [b + side * middle for b in range(middle) for side in range(2)]
    for copy in labels + chunks[order[0]] + chunks[order[1]] + sides:
        copy.start()

    flat = exact(table[...], table_spread(table.shape[1]))
    for rj in range(WIN):
        span_b[pl.ds(rj, HEADS, stride=WIN), :] = exact(flat, row_spread(rj), NT)
    for cj in range(WIN):
        span_a[pl.ds(cj, HEADS * WIN, stride=WIN), :] = exact(span_b[...], col_spread(cj), NT)
    for h in range(HEADS):
        bias_t[:, h * SPAN : (h + 1) * SPAN] = span_a[h * SPAN : (h + 1) * SPAN, :]
    mask_row = iota((LANES, C), 0) >> 6
    mask_col = iota((LANES, C), 1)
    hmask[...] = (
        (mask_col >= mask_row * HEAD) & (mask_col < (mask_row + 1) * HEAD)
    ).astype(F32).astype(BF16)
    score_acc[...] = jnp.zeros_like(score_acc)
    pack[...] = jnp.zeros_like(pack)

    nt_s[...] = jnp.ones_like(nt_s)
    for cj in range(WIN):
        fold_a[cj * SPAN : (cj + 1) * SPAN, :] = col_spread(cj).astype(BF16)
    for rj in range(WIN):
        fold_b[rj * 128 : (rj + 1) * 128, :] = row_spread(rj).astype(BF16)
    weights = qkvw[...]
    offsets = qkvb[...]
    for i in range(3):
        w_s[i] = weights[:, i * C : (i + 1) * C]
        b_s[i] = offsets[:, i * C : (i + 1) * C]

    for copy in labels:
        copy.wait()

    own = reg[...]
    row_left = jnp.concatenate([own[SHIFT:], reg_b[0:SHIFT, :]], 0)[:, 0:1] >> 2
    row_right = jnp.concatenate([reg_a[SHIFT:WIN, :], own[0:SHIFT]], 0)[:, 0:1] >> 2
    row_part = jnp.where(
        iota((WIN, tile_cols), 1) < middle * span_cols,
        jnp.broadcast_to(row_left, (WIN, tile_cols)),
        jnp.broadcast_to(row_right, (WIN, tile_cols)),
    )
    col_own = pltpu.roll(own, tile_cols - SHIFT, 1)
    col_right = pltpu.roll(reg_r[...], tile_cols - SHIFT, 1)
    col_part = jnp.where(iota((WIN, tile_cols), 1) < tile_cols - SHIFT, col_own, col_right)[0:1] & 3
    label = (row_part * 4 + col_part).astype(F32)
    spread = jnp.broadcast_to(label[:, None, :], (WIN, WIN, tile_cols)).reshape(SPAN, tile_cols)
    spread = jnp.where(
        (iota((SPAN, tile_cols), 0) & 7) == (iota((SPAN, tile_cols), 1) & 7), spread, 0.0
    )
    pick = ((iota((tile_cols, wins), 0) >> 3) == iota((tile_cols, wins), 1)).astype(F32)
    columns = exact(spread, pick)
    tiled = (iota((SPAN, LANES), 0) == (iota((SPAN, LANES), 1) & (SPAN - 1))).astype(F32)
    lab_row[...] = exact(columns, tiled, TN)
    for w in range(wins):
        lab_col[w] = jnp.broadcast_to(columns[:, w : w + 1], (SPAN, 128))

    def gather_heads(stacked):
        kept = stacked * hmask[...].astype(F32)
        return jnp.sum(kept.reshape(HEADS, SPAN, C), 0)

    small = 4 * BLOCK
    edge = tile_cols - EDGE
    cut = middle * span_cols
    backs = []

    def back(src, dst, to_row, to_col):
        i = len(backs)
        backs.append(remote(src, dst, back_send.at[i], back_recv.at[i], to_row, to_col))
        backs[-1].start()

    for place, b in enumerate(order):
        for copy in chunks[b] + (sides if b == steps - 1 else []):
            copy.wait()
        if place + 2 < steps:
            for copy in chunks[order[place + 2]]:
                copy.start()
        at = slice(b * step, (b + 1) * step)
        win_at = slice(b * step_wins, (b + 1) * step_wins)
        cols = slice(b * span_cols, (b + 1) * span_cols)
        near = slice(b * span_cols, min((b + 1) * span_cols + EDGE, tile_cols))

        for main, below, above, right, diag, target in (
            (tok, tok_b, tok_a, tok_r, tok_d, unit),
            (grad, grad_b, grad_a, grad_r, grad_d, gradf),
        ):
            for r in range(WIN):
                if b < middle:
                    part = main[r + SHIFT, near] if r < SHIFT else below[r - SHIFT, near]
                else:
                    part = above[r, near] if r < SHIFT else main[r - SHIFT, near]
                wide = part.astype(F32)
                if b == steps - 1:
                    beyond = diag[r] if r < SHIFT else right[r - SHIFT]
                    wide = jnp.concatenate([wide, beyond.astype(F32)], 0)
                target[win_at, r] = wide[SHIFT : SHIFT + span_cols].reshape(step_wins, WIN, C)

        x = unit[win_at].reshape(step, C)
        center = jnp.mean(x, -1, keepdims=True)
        x = x - center
        inv = lax.rsqrt(jnp.mean(x * x, -1, keepdims=True) + 1e-05)
        x = x * inv
        unit[win_at] = x.reshape(step_wins, WIN, WIN, C)
        inv_std[at] = inv
        n = (x * gain_ref[...] + offset_ref[...]).astype(BF16)
        nt_s[0:C, at] = n.T
        q_s[at] = ((mul(n, w_s[0]) + b_s[0]) * HEAD ** (-0.5)).astype(BF16)
        k_s[at] = (mul(n, w_s[1]) + b_s[1]).astype(BF16)
        v_s[at] = (mul(n, w_s[2]) + b_s[2]).astype(BF16)
        g = gradf[win_at].reshape(step, C).astype(BF16)
        gb_s[at] = g
        da_s[at] = mul(g, projw[...], NT).astype(BF16)

        @pl.loop(0, step_wins // 2)
        def _(pair_at):
            loaded = []
            for i in range(2):
                w = b * step_wins + pair_at * 2 + i
                at = pl.ds(pl.multiple_of(w * SPAN, SPAN), SPAN)
                same = lab_col[w][:, 0:1] == lab_row[pl.ds(w, 1), :]
                loaded.append((at, q_s[at], k_s[at], v_s[at], da_s[at], same))
            heads = hmask[...]
            bias = bias_t[...]
            total = score_acc[...]
            for at, q, k, v, da, same in loaded:
                qm = jnp.concatenate([q] * HEADS, 0) * heads
                dam = jnp.concatenate([da] * HEADS, 0) * heads
                scores = jnp.where(same, mul(k, qm, NT) + bias, MASKED)
                e = jnp.exp(scores - jnp.max(scores, 0, keepdims=True))
                p = e * (1.0 / jnp.sum(e, 0, keepdims=True))
                p_low = p.astype(BF16)
                att[at] = gather_heads(mul(p_low, v, TN)).astype(BF16)
                dp = mul(v, dam, NT)
                ds = p * (dp - jnp.sum(p * dp, 0, keepdims=True))
                total += ds
                ds_low = ds.astype(BF16)
                dq_s[at] = (gather_heads(mul(ds_low, k, TN)) * HEAD ** (-0.5)).astype(BF16)
                dk_s[at] = mul(ds_low, qm).astype(BF16)
                dv_s[at] = mul(p_low, dam).astype(BF16)
            score_acc[...] = total

        x = unit[win_at].reshape(step, C)
        dn = mul(dq_s[at], w_s[0], NT) + mul(dk_s[at], w_s[1], NT) + mul(dv_s[at], w_s[2], NT)
        pack[small + 3 : small + 4, 0:C] += jnp.sum(dn * x, 0, keepdims=True)
        pack[small + 4 : small + 5, 0:C] += jnp.sum(dn, 0, keepdims=True)
        g = dn * gain_ref[...]
        dx = inv_std[at] * (
            g - jnp.mean(g, -1, keepdims=True) - x * jnp.mean(g * x, -1, keepdims=True)
        )
        out = (gradf[win_at].reshape(step, C) + dx).reshape(step_wins, WIN, WIN, C)
        for r in range(WIN):
            frame_low[r, cols] = out[:, r].reshape(span_cols, C).astype(BF16)
        if b < middle:
            back(frame_low.at[SHIFT:WIN, cols], back_u.at[0:SHIFT, cols], down, col)
        else:
            back(frame_low.at[0:SHIFT, cols], back_u.at[0:SHIFT, cols], up, col)
        if b == steps - 1:
            back(frame_low.at[SHIFT:WIN, edge:tile_cols], back_l, row, other)
            back(frame_low.at[0:SHIFT, edge:tile_cols], back_ul, up, other)

    for i, part in enumerate((dq_s, dk_s, dv_s)):
        pack[i * BLOCK : (i + 1) * BLOCK, 0:C] = mul(nt_s[...], part[...])[0:BLOCK]
    pack[3 * BLOCK : 3 * BLOCK + C, 0:C] = mul(att[...], gb_s[...], TN)
    for h in range(HEADS):
        span_a[h * SPAN : (h + 1) * SPAN, :] = score_acc[:, h * SPAN : (h + 1) * SPAN]
    wide = jnp.concatenate(
        [span_a[pl.ds(cj, HEADS * WIN, stride=WIN), :] for cj in range(WIN)], 1
    )
    span_b[...] = split_mul(wide, fold_a[...])
    wide = jnp.concatenate(
        [span_b[pl.ds(rj, HEADS, stride=WIN), :] for rj in range(WIN)], 1
    )
    flat_sum = split_mul(wide, fold_b[...])
    pack[small + 8 : small + 8 + HEADS, :] = flat_sum
    pack_low[...] = pack[...].astype(BF16)

    pair = remote(
        pack_low.at[pl.ds(pl.multiple_of(other * half, 16), half)], pair_in,
        pair_sem.at[0], pair_sem.at[1], row, other,
    )
    pair.start()
    pair.wait()
    mine = pl.ds(pl.multiple_of(col * half, 16), half)
    half_low[...] = (pack[mine] + pair_in[...].astype(F32)).astype(BF16)

    def part_copy(k):
        peer = lax.rem(row + k, rows_n)
        return remote(
            half_low.at[pl.ds(pl.multiple_of(peer * chunk, 16), chunk)], part_in.at[k],
            part_send.at[k], part_recv.at[k], peer, col,
        )

    @pl.loop(1, rows_n)
    def _(k):
        part_copy(k).start()

    for copy in backs:
        copy.wait()
    for r in range(WIN):
        if r < SHIFT:
            pieces = (back_l[r], back_u[r, 0:cut], frame_low[r + SHIFT, cut:tile_cols])
        else:
            pieces = (
                back_ul[r - SHIFT], frame_low[r - SHIFT, 0:cut], back_u[r - SHIFT, cut:tile_cols]
            )
        wide = jnp.concatenate([piece.astype(F32) for piece in pieces], 0)
        d_tok[r] = wide[EDGE - SHIFT : EDGE - SHIFT + tile_cols].astype(BF16)

    def add_part(k, total):
        part_copy(k).wait()
        return total + part_in[k].astype(F32)

    my_chunk = pl.ds(pl.multiple_of(row * chunk, 16), chunk)
    total = lax.fori_loop(1, rows_n, add_part, half_low[my_chunk].astype(F32))
    own_chunk = result.at[col, my_chunk]
    own_chunk[...] = total.astype(BF16)

    def all_copy(k):
        return remote(
            own_chunk, own_chunk, all_send.at[k], all_recv.at[k],
            lax.rem(row + k, rows_n), col,
        )

    def forward(k):
        source = lax.rem(row + rows_n - k, rows_n)
        piece = result.at[col, pl.ds(pl.multiple_of(source * chunk, 16), chunk)]
        return remote(piece, piece, fwd_send.at[k], fwd_recv.at[k], row, other)

    @pl.loop(1, rows_n)
    def _(k):
        all_copy(k).start()

    forward(0).start()

    @pl.loop(1, rows_n)
    def _(k):
        all_copy(k).wait()
        forward(k).start()

    @pl.loop(0, rows_n)
    def _(k):
        forward(k).wait()

    pack[0:half] = result[0].astype(F32) * out_scale
    pack[half : 2 * half] = result[1].astype(F32) * out_scale
    d_qkvw[...] = jnp.concatenate(
        [pack[i * BLOCK : i * BLOCK + C, 0:C] for i in range(3)], 1
    )
    d_qkvb[...] = jnp.concatenate(
        [pack[i * BLOCK + C : i * BLOCK + C + 1, 0:C] for i in range(3)], 1
    )
    d_projw[...] = pack[3 * BLOCK : 3 * BLOCK + C, 0:C]
    d_gain[...] = pack[small + 3 : small + 4, 0:C]
    d_offset[...] = pack[small + 4 : small + 5, 0:C]
    entries = table_spread(d_table.shape[1])
    d_table[...] = exact(pack[small + 8 : small + 8 + HEADS, :], entries, NT)


def on_device(
    tokens, grad_out, regions, ln_gain, ln_offset, qkv_weight, qkv_bias, proj_weight, bias_table
):
    rows_n, cols_n = lax.axis_size("row"), lax.axis_size("col")
    tile_cols = tokens.shape[1]
    wins = tile_cols // WIN
    count = wins * SPAN
    steps = wins // 4
    unit_rows = 2 * 16 * rows_n
    needed = 4 * BLOCK + 16
    rows_total = -(-needed // unit_rows) * unit_rows
    half = rows_total // 2
    chunk = half // rows_n
    total_tokens = tokens.shape[0] * tile_cols * rows_n * cols_n
    vmem = pltpu.VMEM
    halo = [
        vmem((SHIFT, tile_cols, C), BF16),
        vmem((SHIFT, EDGE, C), BF16),
        vmem((SHIFT, EDGE, C), BF16),
    ]
    flat_low = vmem((count, C), BF16)
    whole = pl.BlockSpec(memory_space=pltpu.VMEM)
    dma = pltpu.SemaphoreType.DMA
    outs = pl.pallas_call(
        functools.partial(body, rows_n, cols_n, rows_total, total_tokens ** (-0.5)),
        out_shape=(
            jax.ShapeDtypeStruct(tokens.shape, BF16),
            jax.ShapeDtypeStruct((C, 3 * C), F32),
            jax.ShapeDtypeStruct((1, 3 * C), F32),
            jax.ShapeDtypeStruct((C, C), F32),
            jax.ShapeDtypeStruct((HEADS, bias_table.shape[0]), F32),
            jax.ShapeDtypeStruct((1, C), F32),
            jax.ShapeDtypeStruct((1, C), F32),
        ),
        in_specs=[whole] * 9,
        out_specs=(whole,) * 7,
        scratch_shapes=halo + halo + [
            halo[0],
            halo[0],
            vmem(regions.shape, jnp.int32),
            vmem(regions.shape, jnp.int32),
            vmem(regions.shape, jnp.int32),
            vmem((wins, WIN, WIN, C), F32),
            vmem((count, 1), F32),
            vmem((wins, WIN, WIN, C), F32),
            vmem((192, count), BF16),
        ] + [flat_low] * 9 + [
            vmem((3, C, C), BF16),
            vmem((3, 1, C), F32),
            vmem((SPAN, LANES), F32),
            vmem((HEADS * SPAN, SPAN), F32),
            vmem((HEADS * WIN, 128), F32),
            vmem((LANES, C), BF16),
            vmem((wins, SPAN, 128), F32),
            vmem((wins, LANES), F32),
            vmem((SPAN, LANES), F32),
            vmem((WIN * SPAN, 128), BF16),
            vmem((WIN * 128, 256), BF16),
            vmem((WIN, tile_cols, C), BF16),
        ] + halo + [
            vmem((rows_total, 256), F32),
            vmem((rows_total, 256), BF16),
            vmem((half, 256), BF16),
            vmem((half, 256), BF16),
            vmem((rows_n, chunk, 256), BF16),
            vmem((2, half, 256), BF16),
            dma((7 + 2 * steps,)), dma((7 + 2 * steps,)),
            dma((steps + 2,)), dma((steps + 2,)), dma((2,)),
            dma((rows_n,)), dma((rows_n,)), dma((rows_n,)), dma((rows_n,)),
            dma((rows_n,)), dma((rows_n,)),
        ],
        compiler_params=pltpu.CompilerParams(
            collective_id=0, has_side_effects=True, vmem_limit_bytes=48 * 1024 * 1024
        ),
    )(
        tokens, grad_out, regions, ln_gain.reshape(1, C), ln_offset.reshape(1, C), qkv_weight,
        qkv_bias.reshape(1, 3 * C), proj_weight, bias_table.T,
    )
    d_tokens, d_qkvw, d_qkvb, d_projw, d_table, d_gain, d_offset = outs
    return (
        d_tokens,
        d_qkvw,
        d_qkvb.reshape(3 * C),
        d_projw,
        d_table.T,
        d_gain.reshape(C),
        d_offset.reshape(C),
    )


def solution(mesh):
    placed = (
        P(("grp", "row"), "col", None),
        P(("grp", "row"), "col", None),
        P(("grp", "row"), "col"),
        P(),
        P(),
        P(),
        P(),
        P(),
        P(),
    )
    return jax.shard_map(
        on_device,
        mesh=mesh,
        in_specs=placed,
        out_specs=(
            P(("grp", "row"), "col", None),
            P("grp", None),
            P("grp"),
            P("grp", None),
            P("grp", None),
            P("grp"),
            P("grp"),
        ),
        check_vma=False,
    )
```

```python
import functools

import jax
import jax.numpy as jnp
from jax import lax
from jax.experimental import pallas as pl
from jax.experimental.pallas import tpu as pltpu
from jax.sharding import PartitionSpec as P

HEADS = 6
WIN = 8
SHIFT = 4
SPAN = WIN * WIN
C = 180
HEAD = C // HEADS
LANES = HEADS * SPAN
BLOCK = 184
EDGE = 16
MASKED = -10000.0
MESH = pl.DeviceIdType.MESH
F32 = jnp.float32
BF16 = jnp.bfloat16

NN = (((1,), (0,)), ((), ()))
NT = (((1,), (1,)), ((), ()))
TN = (((0,), (0,)), ((), ()))


def mul(left, right, form=NN):
    return lax.dot_general(left, right, form, preferred_element_type=F32)


def exact(left, right, form=NN):
    return lax.dot_general(
        left, right, form, preferred_element_type=F32, precision=lax.Precision.HIGHEST
    )


def split_mul(left, picks):
    high = left.astype(BF16)
    low = (left - high.astype(F32)).astype(BF16)
    return mul(high, picks) + mul(low, picks)


def iota(shape, dim):
    return lax.broadcasted_iota(jnp.int32, shape, dim)


def col_spread(cj):
    src = iota((SPAN, 128), 0)
    dst = iota((SPAN, 128), 1)
    return (dst == (src >> 3) * 16 + (src & 7) - cj + 7).astype(F32)


def row_spread(rj):
    src = iota((128, 256), 0)
    dst = iota((128, 256), 1)
    return (dst == src + 16 * (7 - rj)).astype(F32)


def table_spread(entries):
    src = iota((entries, 256), 0)
    dst = iota((entries, 256), 1)
    hit = (src == (dst >> 4) * 15 + (dst & 15)) & ((dst & 15) < 15) & (dst < 240)
    return hit.astype(F32)


def body(
    rows_n, cols_n, rows_total, out_scale,
    both, reg, gain_ref, offset_ref, qkvw, qkvb, projw, table,
    d_tok, d_qkvw, d_qkvb, d_projw, d_table, d_gain, d_offset,
    both_b, both_r, both_d, reg_b, reg_r,
    unit, inv_std, gradf, nt_s, q_s, k_s, v_s, da_s, gb_s, att, dq_s, dk_s, dv_s,
    w_s, b_s, bias_t, span_a, span_b, hmask, lab_col, lab_row, score_acc,
    fold_a, fold_b, frame_low, frame_two, back_u, back_l, back_ul,
    pack, pack_low, pair_in, half_low, part_in, result,
    halo_send, halo_recv, back_send, back_recv, pair_sem,
    part_send, part_recv, all_send, all_recv, fwd_send, fwd_recv,
):
    row = lax.axis_index("row")
    col = lax.axis_index("col")
    up = lax.rem(row + rows_n - 1, rows_n)
    down = lax.rem(row + 1, rows_n)
    other = lax.rem(col + 1, cols_n)
    tile_cols = both.shape[1]
    wins = tile_cols // WIN
    count = wins * SPAN
    half = rows_total // 2
    chunk = half // rows_n

    def remote(src, dst, send, recv, to_row, to_col):
        return pltpu.make_async_remote_copy(
            src_ref=src, dst_ref=dst, send_sem=send, recv_sem=recv,
            device_id={"row": to_row, "col": to_col}, device_id_type=MESH,
        )

    barrier = pltpu.get_barrier_semaphore()

    @pl.loop(1, rows_n)
    def _(k):
        pl.semaphore_signal(
            barrier, inc=1, device_id={"row": lax.rem(row + k, rows_n), "col": col},
            device_id_type=MESH,
        )

    for to_row in (row, up, down):
        pl.semaphore_signal(
            barrier, inc=1, device_id={"row": to_row, "col": other}, device_id_type=MESH
        )
    pl.semaphore_wait(barrier, rows_n + 2)

    step_wins = 4
    step = step_wins * SPAN
    steps = wins // step_wins
    span_cols = step_wins * WIN

    def halo(i, src, dst, to_row, to_col):
        return remote(src, dst, halo_send.at[i], halo_recv.at[i], to_row, to_col)

    labels = [halo(0, reg, reg_b, up, col), halo(1, reg, reg_r, row, other)]
    sides = [
        halo(2, both.at[SHIFT:WIN, 0:EDGE], both_r, row, other),
        halo(3, both.at[0:SHIFT, 0:EDGE], both_d, up, other),
    ]
    chunks = []
    for b in range(steps):
        first = b * span_cols + (EDGE if b else 0)
        last = min((b + 1) * span_cols + EDGE, tile_cols)
        src, dst = both.at[0:SHIFT, first:last], both_b.at[0:SHIFT, first:last]
        chunks.append([halo(4 + b, src, dst, up, col)])
    for copy in labels + chunks[0] + sides + chunks[1]:
        copy.start()

    flat = exact(table[...], table_spread(table.shape[1]))
    for rj in range(WIN):
        span_b[pl.ds(rj, HEADS, stride=WIN), :] = exact(flat, row_spread(rj), NT)
    for cj in range(WIN):
        span_a[pl.ds(cj, HEADS * WIN, stride=WIN), :] = exact(span_b[...], col_spread(cj), NT)
    for h in range(HEADS):
        bias_t[:, h * SPAN : (h + 1) * SPAN] = span_a[h * SPAN : (h + 1) * SPAN, :]
    mask_row = iota((LANES, C), 0) >> 6
    mask_col = iota((LANES, C), 1)
    hmask[...] = (
        (mask_col >= mask_row * HEAD) & (mask_col < (mask_row + 1) * HEAD)
    ).astype(F32).astype(BF16)
    score_acc[...] = jnp.zeros_like(score_acc)
    pack[...] = jnp.zeros_like(pack)

    nt_s[...] = jnp.ones_like(nt_s)
    for cj in range(WIN):
        fold_a[cj * SPAN : (cj + 1) * SPAN, :] = col_spread(cj).astype(BF16)
    for rj in range(WIN):
        fold_b[rj * 128 : (rj + 1) * 128, :] = row_spread(rj).astype(BF16)
    weights = qkvw[...]
    offsets = qkvb[...]
    for i in range(3):
        w_s[i] = weights[:, i * C : (i + 1) * C]
        b_s[i] = offsets[:, i * C : (i + 1) * C]

    for copy in labels:
        copy.wait()

    own = reg[...]
    row_part = jnp.concatenate([own[SHIFT:], reg_b[0:SHIFT, :]], 0)[:, 0:1] >> 2
    col_own = pltpu.roll(own, tile_cols - SHIFT, 1)
    col_right = pltpu.roll(reg_r[...], tile_cols - SHIFT, 1)
    col_part = jnp.where(iota((WIN, tile_cols), 1) < tile_cols - SHIFT, col_own, col_right)[0:1] & 3
    label = (row_part * 4 + col_part).astype(F32)
    spread = jnp.broadcast_to(label[:, None, :], (WIN, WIN, tile_cols)).reshape(SPAN, tile_cols)
    spread = jnp.where(
        (iota((SPAN, tile_cols), 0) & 7) == (iota((SPAN, tile_cols), 1) & 7), spread, 0.0
    )
    pick = ((iota((tile_cols, wins), 0) >> 3) == iota((tile_cols, wins), 1)).astype(F32)
    columns = exact(spread, pick)
    tiled = (iota((SPAN, LANES), 0) == (iota((SPAN, LANES), 1) & (SPAN - 1))).astype(F32)
    lab_row[...] = exact(columns, tiled, TN)
    for w in range(wins):
        lab_col[w] = jnp.broadcast_to(columns[:, w : w + 1], (SPAN, 128))

    def gather_heads(stacked):
        kept = stacked * hmask[...].astype(F32)
        return jnp.sum(kept.reshape(HEADS, SPAN, C), 0)

    small = 4 * BLOCK
    edge = tile_cols - EDGE
    backs = []

    def back(src, dst, to_row, to_col):
        i = len(backs)
        backs.append(remote(src, dst, back_send.at[i], back_recv.at[i], to_row, to_col))
        backs[-1].start()

    for b in range(steps):
        for copy in chunks[b] + (sides if b == steps - 1 else []):
            copy.wait()
        if b + 2 < steps:
            for copy in chunks[b + 2]:
                copy.start()
        at = slice(b * step, (b + 1) * step)
        win_at = slice(b * step_wins, (b + 1) * step_wins)
        cols = slice(b * span_cols, (b + 1) * span_cols)
        near = slice(b * span_cols, min((b + 1) * span_cols + EDGE, tile_cols))

        for r in range(WIN):
            if r < SHIFT:
                part, beyond = both[r + SHIFT, near], both_r[r]
            else:
                part, beyond = both_b[r - SHIFT, near], both_d[r - SHIFT]
            wide = part.astype(F32)
            if b == steps - 1:
                wide = jnp.concatenate([wide, beyond.astype(F32)], 0)
            wide = wide[SHIFT : SHIFT + span_cols]
            unit[win_at, r] = wide[:, 0:C].reshape(step_wins, WIN, C)
            gradf[win_at, r] = wide[:, C : 2 * C].reshape(step_wins, WIN, C)

        x = unit[win_at].reshape(step, C)
        center = jnp.mean(x, -1, keepdims=True)
        x = x - center
        inv = lax.rsqrt(jnp.mean(x * x, -1, keepdims=True) + 1e-05)
        x = x * inv
        unit[win_at] = x.reshape(step_wins, WIN, WIN, C)
        inv_std[at] = inv
        n = (x * gain_ref[...] + offset_ref[...]).astype(BF16)
        nt_s[0:C, at] = n.T
        q_s[at] = ((mul(n, w_s[0]) + b_s[0]) * HEAD ** (-0.5)).astype(BF16)
        k_s[at] = (mul(n, w_s[1]) + b_s[1]).astype(BF16)
        v_s[at] = (mul(n, w_s[2]) + b_s[2]).astype(BF16)
        g = gradf[win_at].reshape(step, C).astype(BF16)
        gb_s[at] = g
        da_s[at] = mul(g, projw[...], NT).astype(BF16)

        @pl.loop(0, step_wins // 2)
        def _(pair_at):
            loaded = []
            for i in range(2):
                w = b * step_wins + pair_at * 2 + i
                at = pl.ds(pl.multiple_of(w * SPAN, SPAN), SPAN)
                same = lab_col[w][:, 0:1] == lab_row[pl.ds(w, 1), :]
                loaded.append((at, q_s[at], k_s[at], v_s[at], da_s[at], same))
            heads = hmask[...]
            bias = bias_t[...]
            total = score_acc[...]
            for at, q, k, v, da, same in loaded:
                qm = jnp.concatenate([q] * HEADS, 0) * heads
                dam = jnp.concatenate([da] * HEADS, 0) * heads
                scores = jnp.where(same, mul(k, qm, NT) + bias, MASKED)
                e = jnp.exp(scores - jnp.max(scores, 0, keepdims=True))
                p = e * (1.0 / jnp.sum(e, 0, keepdims=True))
                p_low = p.astype(BF16)
                att[at] = gather_heads(mul(p_low, v, TN)).astype(BF16)
                dp = mul(v, dam, NT)
                ds = p * (dp - jnp.sum(p * dp, 0, keepdims=True))
                total += ds
                ds_low = ds.astype(BF16)
                dq_s[at] = (gather_heads(mul(ds_low, k, TN)) * HEAD ** (-0.5)).astype(BF16)
                dk_s[at] = mul(ds_low, qm).astype(BF16)
                dv_s[at] = mul(p_low, dam).astype(BF16)
            score_acc[...] = total

        x = unit[win_at].reshape(step, C)
        dn = mul(dq_s[at], w_s[0], NT) + mul(dk_s[at], w_s[1], NT) + mul(dv_s[at], w_s[2], NT)
        pack[small + 3 : small + 4, 0:C] += jnp.sum(dn * x, 0, keepdims=True)
        pack[small + 4 : small + 5, 0:C] += jnp.sum(dn, 0, keepdims=True)
        g = dn * gain_ref[...]
        dx = inv_std[at] * (
            g - jnp.mean(g, -1, keepdims=True) - x * jnp.mean(g * x, -1, keepdims=True)
        )
        out = (gradf[win_at].reshape(step, C) + dx).reshape(step_wins, WIN, WIN, C)
        for r in range(SHIFT):
            frame_low[r, cols] = out[:, r].reshape(span_cols, C).astype(BF16)
        for r in range(0, SHIFT, 2):
            two = [out[:, SHIFT + r + i].reshape(span_cols, C) for i in range(2)]
            frame_two[r // 2, cols] = jnp.concatenate(two, 1).astype(BF16)
        back(frame_two.at[0:2, cols], back_u.at[0:2, cols], down, col)
        if b == steps - 1:
            back(frame_low.at[0:SHIFT, edge:tile_cols], back_l, row, other)
            back(frame_two.at[0:2, edge:tile_cols], back_ul, down, other)

    for i, part in enumerate((dq_s, dk_s, dv_s)):
        pack[i * BLOCK : (i + 1) * BLOCK, 0:C] = mul(nt_s[...], part[...])[0:BLOCK]
    pack[3 * BLOCK : 3 * BLOCK + C, 0:C] = mul(att[...], gb_s[...], TN)
    for h in range(HEADS):
        span_a[h * SPAN : (h + 1) * SPAN, :] = score_acc[:, h * SPAN : (h + 1) * SPAN]
    wide = jnp.concatenate(
        [span_a[pl.ds(cj, HEADS * WIN, stride=WIN), :] for cj in range(WIN)], 1
    )
    span_b[...] = split_mul(wide, fold_a[...])
    wide = jnp.concatenate(
        [span_b[pl.ds(rj, HEADS, stride=WIN), :] for rj in range(WIN)], 1
    )
    flat_sum = split_mul(wide, fold_b[...])
    pack[small + 8 : small + 8 + HEADS, :] = flat_sum
    pack_low[...] = pack[...].astype(BF16)

    pair = remote(
        pack_low.at[pl.ds(pl.multiple_of(other * half, 16), half)], pair_in,
        pair_sem.at[0], pair_sem.at[1], row, other,
    )
    pair.start()
    pair.wait()
    mine = pl.ds(pl.multiple_of(col * half, 16), half)
    half_low[...] = (pack[mine] + pair_in[...].astype(F32)).astype(BF16)

    def part_copy(k):
        peer = lax.rem(row + k, rows_n)
        return remote(
            half_low.at[pl.ds(pl.multiple_of(peer * chunk, 16), chunk)], part_in.at[k],
            part_send.at[k], part_recv.at[k], peer, col,
        )

    @pl.loop(1, rows_n)
    def _(k):
        part_copy(k).start()

    for copy in backs:
        copy.wait()
    for r in range(WIN):
        if r < SHIFT:
            lanes = slice((r % 2) * C, (r % 2 + 1) * C)
            left_part = back_ul[r // 2].astype(F32)[:, lanes]
            main_part = back_u[r // 2].astype(F32)[:, lanes]
        else:
            left_part, main_part = back_l[r - SHIFT], frame_low[r - SHIFT]
        wide = jnp.concatenate([left_part.astype(F32), main_part.astype(F32)], 0)
        d_tok[r] = wide[EDGE - SHIFT : EDGE - SHIFT + tile_cols].astype(BF16)

    def add_part(k, total):
        part_copy(k).wait()
        return total + part_in[k].astype(F32)

    my_chunk = pl.ds(pl.multiple_of(row * chunk, 16), chunk)
    total = lax.fori_loop(1, rows_n, add_part, half_low[my_chunk].astype(F32))
    own_chunk = result.at[col, my_chunk]
    own_chunk[...] = total.astype(BF16)

    def all_copy(k):
        return remote(
            own_chunk, own_chunk, all_send.at[k], all_recv.at[k],
            lax.rem(row + k, rows_n), col,
        )

    def forward(k):
        source = lax.rem(row + rows_n - k, rows_n)
        piece = result.at[col, pl.ds(pl.multiple_of(source * chunk, 16), chunk)]
        return remote(piece, piece, fwd_send.at[k], fwd_recv.at[k], row, other)

    @pl.loop(1, rows_n)
    def _(k):
        all_copy(k).start()

    forward(0).start()

    @pl.loop(1, rows_n)
    def _(k):
        all_copy(k).wait()
        forward(k).start()

    @pl.loop(0, rows_n)
    def _(k):
        forward(k).wait()

    pack[0:half] = result[0].astype(F32) * out_scale
    pack[half : 2 * half] = result[1].astype(F32) * out_scale
    d_qkvw[...] = jnp.concatenate(
        [pack[i * BLOCK : i * BLOCK + C, 0:C] for i in range(3)], 1
    )
    d_qkvb[...] = jnp.concatenate(
        [pack[i * BLOCK + C : i * BLOCK + C + 1, 0:C] for i in range(3)], 1
    )
    d_projw[...] = pack[3 * BLOCK : 3 * BLOCK + C, 0:C]
    d_gain[...] = pack[small + 3 : small + 4, 0:C]
    d_offset[...] = pack[small + 4 : small + 5, 0:C]
    entries = table_spread(d_table.shape[1])
    d_table[...] = exact(pack[small + 8 : small + 8 + HEADS, :], entries, NT)


def on_device(
    tokens, grad_out, regions, ln_gain, ln_offset, qkv_weight, qkv_bias, proj_weight, bias_table
):
    rows_n, cols_n = lax.axis_size("row"), lax.axis_size("col")
    tile_cols = tokens.shape[1]
    wins = tile_cols // WIN
    count = wins * SPAN
    steps = wins // 4
    unit_rows = 2 * 16 * rows_n
    needed = 4 * BLOCK + 16
    rows_total = -(-needed // unit_rows) * unit_rows
    half = rows_total // 2
    chunk = half // rows_n
    total_tokens = tokens.shape[0] * tile_cols * rows_n * cols_n
    vmem = pltpu.VMEM
    halo = [
        vmem((SHIFT, tile_cols, 2 * C), BF16),
        vmem((SHIFT, EDGE, 2 * C), BF16),
        vmem((SHIFT, EDGE, 2 * C), BF16),
    ]
    home = [
        vmem((SHIFT, tile_cols, C), BF16),
        vmem((2, tile_cols, 2 * C), BF16),
        vmem((2, tile_cols, 2 * C), BF16),
        vmem((SHIFT, EDGE, C), BF16),
        vmem((2, EDGE, 2 * C), BF16),
    ]
    flat_low = vmem((count, C), BF16)
    whole = pl.BlockSpec(memory_space=pltpu.VMEM)
    dma = pltpu.SemaphoreType.DMA
    outs = pl.pallas_call(
        functools.partial(body, rows_n, cols_n, rows_total, total_tokens ** (-0.5)),
        out_shape=(
            jax.ShapeDtypeStruct(tokens.shape, BF16),
            jax.ShapeDtypeStruct((C, 3 * C), F32),
            jax.ShapeDtypeStruct((1, 3 * C), F32),
            jax.ShapeDtypeStruct((C, C), F32),
            jax.ShapeDtypeStruct((HEADS, bias_table.shape[0]), F32),
            jax.ShapeDtypeStruct((1, C), F32),
            jax.ShapeDtypeStruct((1, C), F32),
        ),
        in_specs=[whole] * 8,
        out_specs=(whole,) * 7,
        scratch_shapes=halo + [
            vmem(regions.shape, jnp.int32),
            vmem(regions.shape, jnp.int32),
            vmem((wins, WIN, WIN, C), F32),
            vmem((count, 1), F32),
            vmem((wins, WIN, WIN, C), F32),
            vmem((192, count), BF16),
        ] + [flat_low] * 9 + [
            vmem((3, C, C), BF16),
            vmem((3, 1, C), F32),
            vmem((SPAN, LANES), F32),
            vmem((HEADS * SPAN, SPAN), F32),
            vmem((HEADS * WIN, 128), F32),
            vmem((LANES, C), BF16),
            vmem((wins, SPAN, 128), F32),
            vmem((wins, LANES), F32),
            vmem((SPAN, LANES), F32),
            vmem((WIN * SPAN, 128), BF16),
            vmem((WIN * 128, 256), BF16),
        ] + home + [
            vmem((rows_total, 256), F32),
            vmem((rows_total, 256), BF16),
            vmem((half, 256), BF16),
            vmem((half, 256), BF16),
            vmem((rows_n, chunk, 256), BF16),
            vmem((2, half, 256), BF16),
            dma((4 + steps,)), dma((4 + steps,)),
            dma((steps + 2,)), dma((steps + 2,)), dma((2,)),
            dma((rows_n,)), dma((rows_n,)), dma((rows_n,)), dma((rows_n,)),
            dma((rows_n,)), dma((rows_n,)),
        ],
        compiler_params=pltpu.CompilerParams(
            collective_id=0, has_side_effects=True, vmem_limit_bytes=48 * 1024 * 1024
        ),
    )(
        jnp.concatenate([tokens, grad_out], -1), regions, ln_gain.reshape(1, C), ln_offset.reshape(1, C), qkv_weight,
        qkv_bias.reshape(1, 3 * C), proj_weight, bias_table.T,
    )
    d_tokens, d_qkvw, d_qkvb, d_projw, d_table, d_gain, d_offset = outs
    return (
        d_tokens,
        d_qkvw,
        d_qkvb.reshape(3 * C),
        d_projw,
        d_table.T,
        d_gain.reshape(C),
        d_offset.reshape(C),
    )


def solution(mesh):
    placed = (
        P(("grp", "row"), "col", None),
        P(("grp", "row"), "col", None),
        P(("grp", "row"), "col"),
        P(),
        P(),
        P(),
        P(),
        P(),
        P(),
    )
    return jax.shard_map(
        on_device,
        mesh=mesh,
        in_specs=placed,
        out_specs=(
            P(("grp", "row"), "col", None),
            P("grp", None),
            P("grp"),
            P("grp", None),
            P("grp", None),
            P("grp"),
            P("grp"),
        ),
        check_vma=False,
    )
```
